32 devices in a mesh: groups: 2 (over y), lon: 4 (over z), lat: 2 (over x), segment: 2 (over core).
Axes of the slice: x: 2, y: 2, z: 4, core: 2. Of those that a mesh axis runs over, the one named last changes fastest.
Arguments:
- inputs: bfloat16 [32, 128, 512], P(('groups', 'lat'), 'lon'), parts along dimension 0, may hold values from -6 to 6
- cotangent: bfloat16 [32, 128, 512], P(('groups', 'lat'), 'lon'), parts along dimension 0, may hold values from -8 to 8
- kernel: bfloat16 [2, 49, 512], P('segment'), may hold values from -0.875 to 0.875
- conv_bias: float32 [2, 512], P('segment'), may hold values from -3 to 3
- norm_gain: float32 [2, 512], P('segment'), may hold values from 0.5 to 2
- norm_shift: float32 [2, 512], P('segment'), may hold values from -3 to 3
- up_weight: bfloat16 [2, 512, 2048], P('segment'), may hold values from -0.25 to 0.25
- hidden_bias: float32 [2, 2048], P('segment'), may hold values from -3 to 3
- down_weight: bfloat16 [2, 2048, 512], P('segment'), may hold values from -0.125 to 0.125
- out_bias: float32 [2, 512], P('segment'), may hold values from -3 to 3
- layer_scale: float32 [2, 512], P('segment'), may hold values from 0.5 to 1.5
Outputs:
- section_out: bfloat16 [2, 32, 128, 512], P('segment', ('groups', 'lat'), 'lon'), parts along dimension 1
- boundary_grad: bfloat16 [2, 32, 128, 512], P('segment', ('groups', 'lat'), 'lon'), parts along dimension 1
- up_grad: float32 [4, 512, 2048], P(('groups', 'segment'), None, ('lon', 'lat')), parts along dimension 0
- down_grad: float32 [4, 2048, 512], P(('groups', 'segment'), ('lon', 'lat')), parts along dimension 0
- hidden_bias_grad: float32 [4, 2048], P(('groups', 'segment'), ('lon', 'lat')), parts along dimension 0
- kernel_grad: float32 [4, 49, 512], P(('groups', 'segment'), None, ('lon', 'lat')), parts along dimension 0
- vector_grad: float32 [4, 5, 512], P(('groups', 'segment'), None, ('lon', 'lat')), parts along dimension 0
The draws below stay inside these ranges and needn't reach their ends.
There are 2 independent parts, one for each index of `groups`. The reference program is written for one: setup_inputs(seed, part) draws one part's arguments, and reference() takes and returns one part's arrays. A program takes and returns all parts, laid end to end along the dimension named above; an argument that names none is the same for every part. Nothing has to cross between parts.
All inputs are finite; a program needn't handle non-finite values.
Results may differ from the reference program's by a relative error of at most 0.023.
Values may be sent and summed in bfloat16 or wider, within the bound.
No kernel may reach another device: no remote copies, remote signals or barrier semaphores. Data moves between devices by JAX's collectives and lax.ppermute only.
A program may use at most 128 MiB of HBM per device.

```python
import math
import jax
import jax.numpy as jnp
from jax import lax

C = 512
HID = 2048
KERNEL = 7
SECTIONS = 2
LAT = 16
LON = 128


def spiked(values, own_key, source, target, shards_of, factor):
    def block_of(axis_at):
        return (jnp.arange(values.shape[axis_at]) // (values.shape[axis_at] // shards_of)).reshape((-1,) + (1,) * (values.ndim - 1 - axis_at))

    near = jax.random.permutation(own_key, shards_of)[block_of(target)]
    other_side = (block_of(target) + shards_of // 2) % shards_of
    return jnp.where((block_of(source) == near) | (block_of(source) == other_side), factor * values, values)


def block_scale(own_key, shape, pieces, smallest, high):
    level, own = 1.0, jax.random.fold_in(own_key, 6)
    for axis_at, shards_of in pieces:
        heights = jnp.exp(jax.random.uniform(jax.random.fold_in(own, axis_at), (shards_of,), jnp.float32, smallest / len(pieces), high / len(pieces)))
        level = level * jnp.repeat(heights, shape[axis_at] // shards_of).reshape([-1 if axis == axis_at else 1 for axis in range(len(shape))])
    return level


def scatter_about(stream_key, extent, width, limit, split=(), dtype=jnp.bfloat16):
    gain = block_scale(stream_key, extent, split, -0.22, 0.18) if split else 1.0
    array = jax.random.normal(stream_key, extent, jnp.float32) * width * gain
    return jnp.minimum(jnp.maximum(array, -limit), limit).astype(dtype)


def noise_with(rng, extent, deviation, reach, cuts, heavy, held_as=jnp.bfloat16):
    values = deviation * jax.random.normal(rng, extent, jnp.float32)
    if cuts:
        values = values * block_scale(rng, extent, cuts, -0.22, 0.18)
    return jnp.clip(spiked(values, jax.random.fold_in(rng, 3), *heavy), -reach, reach).astype(held_as)


def setup_inputs(seed: int = 0, part: int = 0) -> dict:
    key_list = jax.random.split(jax.random.key(seed), 12)
    part_keys = jax.random.split(jax.random.fold_in(key_list[11], part), 12)
    inputs = scatter_about(part_keys[0], (LAT, LON, C), 1.0, 6.0, ((0, 2), (1, 4)))
    cotangent = noise_with(part_keys[1], (LAT, LON, C), 1.0, 8.0, ((0, 2), (1, 4)), (1, 2, 4, 2.0))
    kernel = scatter_about(key_list[2], (SECTIONS, KERNEL * KERNEL, C), (KERNEL * KERNEL) ** -0.5, 0.875, ((0, 2),))
    conv_bias = scatter_about(key_list[3], (SECTIONS, C), 0.5, 3.0, ((0, 2),), jnp.float32)
    norm_gain = jnp.clip(jnp.exp(math.log(2.0) - 1.3862944 * jax.random.uniform(key_list[4], (SECTIONS, C), jnp.float32) ** block_scale(key_list[4], (SECTIONS, C), ((0, 2),), -0.2, 0.2)), 0.5, 2.0)
    norm_shift = scatter_about(key_list[5], (SECTIONS, C), 0.5, 3.0, ((0, 2),), jnp.float32)
    up_weight = scatter_about(key_list[6], (SECTIONS, C, HID), C ** -0.5, 0.25, ((0, 2),))
    hidden_bias = scatter_about(key_list[7], (SECTIONS, HID), 0.5, 3.0, ((0, 2),), jnp.float32)
    down_weight = scatter_about(key_list[8], (SECTIONS, HID, C), HID ** -0.5, 0.125, ((0, 2),))
    out_bias = scatter_about(key_list[9], (SECTIONS, C), 0.5, 3.0, ((0, 2),), jnp.float32)
    layer_scale = jnp.clip(0.5 + 1.0 * jax.random.uniform(key_list[10], (SECTIONS, C), jnp.float32) ** block_scale(key_list[10], (SECTIONS, C), ((0, 2),), -0.2, 0.2), 0.5, 1.5)
    return dict(inputs=inputs, cotangent=cotangent, kernel=kernel, conv_bias=conv_bias, norm_gain=norm_gain, norm_shift=norm_shift, up_weight=up_weight, hidden_bias=hidden_bias, down_weight=down_weight, out_bias=out_bias, layer_scale=layer_scale)


EPSILON = 1e-06
ROOT_HALF = 0.7071067811865476
DENSITY_SCALE = 0.3989422804014327

def extend_field(values):
    margin = KERNEL // 2
    half_turn = values.shape[1] // 2
    northern = jnp.roll(values[:margin][::-1], half_turn, axis=1)
    southern = jnp.roll(values[-margin:][::-1], half_turn, axis=1)
    lat_extended = jnp.concatenate([northern, values, southern], axis=0)
    return jnp.concatenate([lat_extended[:, -margin:], lat_extended, lat_extended[:, :margin]], axis=1)

def correlate(padded, stencil, out_rows, out_cols):
    accumulated = jnp.zeros((out_rows, out_cols, padded.shape[2]), jnp.float32)
    for row_tap in range(KERNEL):
        for col_tap in range(KERNEL):
            window = padded[row_tap:row_tap + out_rows, col_tap:col_tap + out_cols].astype(jnp.float32)
            accumulated = accumulated + window * stencil[row_tap, col_tap].astype(jnp.float32)
    return accumulated

def stencil_terms(padded, grad_low, out_rows, out_cols):
    grad_wide = grad_low.astype(jnp.float32)
    columns = []
    for row_tap in range(KERNEL):
        for col_tap in range(KERNEL):
            window = padded[row_tap:row_tap + out_rows, col_tap:col_tap + out_cols].astype(jnp.float32)
            columns.append(lax.optimization_barrier(jnp.sum(window * grad_wide, axis=(0, 1))))
    return jnp.stack(columns)

def gelu_parts(before):
    cumulative = 0.5 * (1.0 + lax.erf(before * ROOT_HALF))
    density = jnp.exp(-0.5 * before * before) * DENSITY_SCALE
    return (before * cumulative, cumulative + before * density)

def forward_section(values, padded, params):
    stencil, conv_bias, norm_gain, norm_shift, up_matrix, bias_hidden, down_matrix, bias_out, scaling = params
    out_rows, out_cols, channels = values.shape
    stencil_grid = stencil.reshape(KERNEL, KERNEL, channels)
    activity = correlate(padded, stencil_grid, out_rows, out_cols) + conv_bias
    average = lax.optimization_barrier(jnp.mean(activity, axis=-1, keepdims=True))
    centred = activity - average
    variance = lax.optimization_barrier(jnp.mean(centred * centred, axis=-1, keepdims=True))
    inverse = lax.rsqrt(variance + EPSILON)
    unit_norm = centred * inverse
    normed = (unit_norm * norm_gain + norm_shift).astype(jnp.bfloat16).reshape(out_rows * out_cols, channels)
    before = jnp.dot(normed, up_matrix, preferred_element_type=jnp.float32) + bias_hidden
    activated, slope_value = gelu_parts(before)
    hidden = activated.astype(jnp.bfloat16)
    branch = jnp.dot(hidden, down_matrix, preferred_element_type=jnp.float32) + bias_out
    result = (values.astype(jnp.float32) + scaling * branch.reshape(out_rows, out_cols, channels)).astype(jnp.bfloat16)
    return (result, (padded, unit_norm, inverse, normed, slope_value, hidden, branch))

def backward_section(stored, upstream, params, extender, north_weight, south_weight):
    padded, unit_norm, inverse, normed, slope_value, hidden, branch = stored
    stencil, conv_bias, norm_gain, norm_shift, up_matrix, bias_hidden, down_matrix, bias_out, scaling = params
    out_rows, out_cols, channels = upstream.shape
    margin = KERNEL // 2
    incoming = upstream.astype(jnp.float32)
    incoming_flat = incoming.reshape(out_rows * out_cols, channels)
    scale_grad = lax.optimization_barrier(jnp.sum(incoming_flat * branch, axis=0))
    scaled = (incoming_flat * scaling).astype(jnp.bfloat16)
    bias_out_grad = lax.optimization_barrier(jnp.sum(scaled.astype(jnp.float32), axis=0))
    down_sum = jnp.dot(hidden.T, scaled, preferred_element_type=jnp.float32)
    hidden_grad = jnp.dot(scaled, down_matrix.T, preferred_element_type=jnp.float32)
    before_grad = (hidden_grad * slope_value).astype(jnp.bfloat16)
    up_sum = jnp.dot(normed.T, before_grad, preferred_element_type=jnp.float32)
    bias_sum = lax.optimization_barrier(jnp.sum(before_grad.astype(jnp.float32), axis=0))
    normed_grad = jnp.dot(before_grad, up_matrix.T, preferred_element_type=jnp.float32).reshape(out_rows, out_cols, channels)
    gain_grad = lax.optimization_barrier(jnp.sum(normed_grad * unit_norm, axis=(0, 1)))
    shift_grad = lax.optimization_barrier(jnp.sum(normed_grad, axis=(0, 1)))
    gained = normed_grad * norm_gain
    activity_grad = inverse * (gained - lax.optimization_barrier(jnp.mean(gained, axis=-1, keepdims=True)) - unit_norm * lax.optimization_barrier(jnp.mean(gained * unit_norm, axis=-1, keepdims=True)))
    activity_low = activity_grad.astype(jnp.bfloat16)
    conv_bias_grad = lax.optimization_barrier(jnp.sum(activity_low.astype(jnp.float32), axis=(0, 1)))
    stencil_sum = stencil_terms(padded, activity_low, out_rows, out_cols)
    spread = extender(activity_low)
    stencil_grid = stencil.reshape(KERNEL, KERNEL, channels).astype(jnp.float32)
    flipped = stencil_grid[::-1, ::-1]
    correction = stencil_grid[:, ::-1] - flipped
    through = correlate(spread, flipped, out_rows, out_cols)
    zero_rows = jnp.zeros_like(spread[:2 * margin])
    top_part = jnp.concatenate([spread[:margin], zero_rows], axis=0)
    bottom_part = jnp.concatenate([zero_rows, spread[-margin:]], axis=0)
    top_fix = correlate(top_part, correction, margin, out_cols) * north_weight
    bottom_fix = correlate(bottom_part, correction, margin, out_cols) * south_weight
    rest_rows = out_rows - margin
    top_full = jnp.pad(top_fix, ((0, rest_rows), (0, 0), (0, 0)))
    bottom_full = jnp.pad(bottom_fix, ((rest_rows, 0), (0, 0), (0, 0)))
    through = through + top_full + bottom_full
    passed = (incoming + through).astype(jnp.bfloat16)
    vectors = jnp.stack([conv_bias_grad, gain_grad, shift_grad, bias_out_grad, scale_grad])
    return (passed, (up_sum, down_sum, bias_sum, stencil_sum, vectors))

def reference(inputs, cotangent, kernel, conv_bias, norm_gain, norm_shift, up_weight, hidden_bias, down_weight, out_bias, layer_scale):

    def section_params(index):
        return (kernel[index], conv_bias[index], norm_gain[index], norm_shift[index], up_weight[index], hidden_bias[index], down_weight[index], out_bias[index], layer_scale[index])
    first_out, first_stored = forward_section(inputs, extend_field(inputs), section_params(0))
    second_out, second_stored = forward_section(first_out, extend_field(first_out), section_params(1))
    second_grad, second_sums = backward_section(second_stored, cotangent, section_params(1), extend_field, 1.0, 1.0)
    first_grad, first_sums = backward_section(first_stored, second_grad, section_params(0), extend_field, 1.0, 1.0)
    return (jnp.stack([first_out, second_out]), jnp.stack([first_grad, second_grad]), jnp.stack([first_sums[0], second_sums[0]]), jnp.stack([first_sums[1], second_sums[1]]), jnp.stack([first_sums[2], second_sums[2]]), jnp.stack([first_sums[3], second_sums[3]]), jnp.stack([first_sums[4], second_sums[4]]))
```

```python
import jax
import jax.numpy as jnp
from jax import lax
from jax.sharding import PartitionSpec as P

KERNEL = 7


EPSILON = 1e-06
ROOT_HALF = 0.7071067811865476
DENSITY_SCALE = 0.3989422804014327


def correlate(padded, stencil, out_rows, out_cols):
    accumulated = jnp.zeros((out_rows, out_cols, padded.shape[2]), jnp.float32)
    for row_tap in range(KERNEL):
        for col_tap in range(KERNEL):
            window = padded[row_tap : row_tap + out_rows, col_tap : col_tap + out_cols].astype(
                jnp.float32
            )
            accumulated = accumulated + window * stencil[row_tap, col_tap].astype(jnp.float32)
    return accumulated


def stencil_terms(padded, grad_low, out_rows, out_cols):
    grad_wide = grad_low.astype(jnp.float32)
    columns = []
    for row_tap in range(KERNEL):
        for col_tap in range(KERNEL):
            window = padded[row_tap : row_tap + out_rows, col_tap : col_tap + out_cols].astype(
                jnp.float32
            )
            columns.append(jnp.sum(window * grad_wide, axis=(0, 1)))
    return jnp.stack(columns)


def gelu_parts(before):
    cumulative = 0.5 * (1.0 + lax.erf(before * ROOT_HALF))
    density = jnp.exp(-0.5 * before * before) * DENSITY_SCALE
    return (before * cumulative, cumulative + before * density)


def forward_section(values, padded, params):
    (
        stencil,
        conv_bias,
        norm_gain,
        norm_shift,
        up_matrix,
        bias_hidden,
        down_matrix,
        bias_out,
        scaling,
    ) = params
    out_rows, out_cols, channels = values.shape
    stencil_grid = stencil.reshape(KERNEL, KERNEL, channels)
    activity = correlate(padded, stencil_grid, out_rows, out_cols) + conv_bias
    average = jnp.mean(activity, axis=-1, keepdims=True)
    centred = activity - average
    variance = jnp.mean(centred * centred, axis=-1, keepdims=True)
    inverse = lax.rsqrt(variance + EPSILON)
    unit_norm = centred * inverse
    normed = (
        (unit_norm * norm_gain + norm_shift)
        .astype(jnp.bfloat16)
        .reshape(out_rows * out_cols, channels)
    )
    before = jnp.dot(normed, up_matrix, preferred_element_type=jnp.float32) + bias_hidden
    activated, slope_value = gelu_parts(before)
    hidden = activated.astype(jnp.bfloat16)
    branch = jnp.dot(hidden, down_matrix, preferred_element_type=jnp.float32) + bias_out
    result = (
        values.astype(jnp.float32) + scaling * branch.reshape(out_rows, out_cols, channels)
    ).astype(jnp.bfloat16)
    return (result, (padded, unit_norm, inverse, normed, slope_value, hidden, branch))


def backward_section(stored, upstream, params, extender):
    padded, unit_norm, inverse, normed, slope_value, hidden, branch = stored
    (
        stencil,
        conv_bias,
        norm_gain,
        norm_shift,
        up_matrix,
        bias_hidden,
        down_matrix,
        bias_out,
        scaling,
    ) = params
    out_rows, out_cols, channels = upstream.shape
    margin = KERNEL // 2
    incoming = upstream.astype(jnp.float32)
    incoming_flat = incoming.reshape(out_rows * out_cols, channels)
    scale_grad = jnp.sum(incoming_flat * branch, axis=0)
    scaled = (incoming_flat * scaling).astype(jnp.bfloat16)
    bias_out_grad = jnp.sum(scaled.astype(jnp.float32), axis=0)
    hidden_grad = jnp.dot(scaled, down_matrix.T, preferred_element_type=jnp.float32)
    before_grad = (hidden_grad * slope_value).astype(jnp.bfloat16)
    bias_sum = jnp.sum(before_grad.astype(jnp.float32), axis=0)
    normed_grad = jnp.dot(before_grad, up_matrix.T, preferred_element_type=jnp.float32).reshape(
        out_rows, out_cols, channels
    )
    gain_grad = jnp.sum(normed_grad * unit_norm, axis=(0, 1))
    shift_grad = jnp.sum(normed_grad, axis=(0, 1))
    gained = normed_grad * norm_gain
    activity_grad = inverse * (
        gained
        - jnp.mean(gained, axis=-1, keepdims=True)
        - unit_norm * jnp.mean(gained * unit_norm, axis=-1, keepdims=True)
    )
    activity_low = activity_grad.astype(jnp.bfloat16)
    conv_bias_grad = jnp.sum(activity_low.astype(jnp.float32), axis=(0, 1))
    spread = extender(activity_low)
    stencil_sum = stencil_terms(padded, activity_low, out_rows, out_cols)
    stencil_grid = stencil.reshape(KERNEL, KERNEL, channels).astype(jnp.float32)
    flipped = stencil_grid[::-1, ::-1]
    correction = stencil_grid[:, ::-1] - flipped
    through = correlate(spread, flipped, out_rows, out_cols)
    zero_rows = jnp.zeros_like(spread[: 2 * margin])
    top_part = jnp.concatenate([spread[:margin], zero_rows], axis=0)
    bottom_part = jnp.concatenate([zero_rows, spread[-margin:]], axis=0)
    top_fix = correlate(top_part, correction, margin, out_cols)
    bottom_fix = correlate(bottom_part, correction, margin, out_cols)
    rest_rows = out_rows - margin
    top_full = jnp.pad(top_fix, ((0, rest_rows), (0, 0), (0, 0)))
    bottom_full = jnp.pad(bottom_fix, ((rest_rows, 0), (0, 0), (0, 0)))
    passed = (incoming + through + top_full + bottom_full).astype(jnp.bfloat16)
    vectors = jnp.stack([conv_bias_grad, gain_grad, shift_grad, bias_out_grad, scale_grad])
    return (passed, (normed, before_grad, hidden, scaled), (stencil_sum, vectors, bias_sum))


RING = ("lon", "segment")


def from_ahead(value, axis, steps):
    count = lax.axis_size(axis)
    return lax.ppermute(value, axis, [((i + steps) % count, i) for i in range(count)])


def all_rows(band):
    count = lax.axis_size("lat")
    here = lax.axis_index("lat")
    rows = band.shape[0]
    whole = jnp.zeros((count * rows,) + band.shape[1:], band.dtype)
    for steps in range(count):
        piece = band if steps == 0 else from_ahead(band, "lat", steps)
        whole = lax.dynamic_update_slice_in_dim(whole, piece, (here + steps) % count * rows, 0)
    return whole


def extend_local(values):
    margin = KERNEL // 2
    half = lax.axis_size(RING) // 2
    polar = jnp.concatenate([values[:margin], values[-margin:]], axis=0)
    west = from_ahead(values[:, -margin:], RING, -1)
    east = from_ahead(values[:, :margin], RING, 1)
    beyond = from_ahead(polar, RING, half)
    beyond_west = from_ahead(polar[:, -margin:], RING, half - 1)
    beyond_east = from_ahead(polar[:, :margin], RING, half + 1)
    folded = jnp.concatenate([beyond_west, beyond, beyond_east], axis=1)
    middle = jnp.concatenate([west, values, east], axis=1)
    return jnp.concatenate([folded[:margin][::-1], middle, folded[margin:][::-1]], axis=0)


def other_core(value):
    return lax.ppermute(value, "segment", [(0, 1), (1, 0)])


def own_blocks(sums, blocks):
    lons, lats = lax.axis_size("lon"), lax.axis_size("lat")
    cut = sums.reshape(sums.shape[:-1] + (lons, lats, blocks))
    return lax.dynamic_index_in_dim(cut, lax.axis_index("lat"), cut.ndim - 2, keepdims=False)


def sum_to_owner(partial, section):
    lons = lax.axis_size("lon")
    here = lax.axis_index("lon")
    kind = partial.dtype
    other = lax.ppermute(partial, "segment", [(1 - section, section)])
    chip = partial.astype(jnp.float32) + other.astype(jnp.float32)
    low = chip.astype(kind)
    total = lax.dynamic_index_in_dim(chip, here, 1, keepdims=False)
    for steps in range(1, lons):
        block = lax.dynamic_index_in_dim(low, (here + steps) % lons, 1, keepdims=False)
        pairs = [
            (i * 2 + section, (i + steps) % lons * 2 + section) for i in range(lons)
        ]
        total = total + lax.ppermute(block, RING, pairs).astype(jnp.float32)
    return total


def cell_products(left, right):
    cells, lons, wide = right.shape
    sums = jnp.dot(left.T, right.reshape(cells, -1), preferred_element_type=jnp.float32)
    return sums.astype(jnp.bfloat16).reshape(-1, lons, wide)


def section_sums(matrices, smalls, section):
    normed, before_grad, hidden, scaled = matrices
    stencil_sum, vectors, bias_sum = smalls
    devices = lax.axis_size("lon") * lax.axis_size("lat")
    channels, units = normed.shape[1], hidden.shape[1]
    wide, narrow = units // devices, channels // devices
    down = sum_to_owner(
        cell_products(scaled, own_blocks(hidden, wide)),
        section,
    )
    up = sum_to_owner(
        cell_products(normed, own_blocks(before_grad, wide)),
        section,
    )
    thin = own_blocks(jnp.concatenate([stencil_sum, vectors], axis=0), narrow)
    bias = own_blocks(bias_sum, wide).reshape(thin.shape[1], -1, narrow).transpose(1, 0, 2)
    small = sum_to_owner(jnp.concatenate([thin, bias], axis=0), section)
    taps = stencil_sum.shape[0]
    rows = taps + vectors.shape[0]
    return (up, down.T, small[rows:].reshape(-1), small[:taps], small[taps:rows])


def local(
    inputs,
    cotangent,
    kernel,
    conv_bias,
    norm_gain,
    norm_shift,
    up_weight,
    hidden_bias,
    down_weight,
    out_bias,
    layer_scale,
):
    core = lax.axis_index("segment")
    leading = core == 0
    columns = inputs.shape[1] // 2
    rows = inputs.shape[0]
    own = (
        kernel[0],
        conv_bias[0],
        norm_gain[0],
        norm_shift[0],
        up_weight[0],
        hidden_bias[0],
        down_weight[0],
        out_bias[0],
        layer_scale[0],
    )
    other = jax.tree.map(other_core, own)
    first_params = jax.tree.map(lambda a, b: jnp.where(leading, a, b), own, other)
    second_params = jax.tree.map(lambda a, b: jnp.where(leading, b, a), own, other)

    def mine(field):
        return lax.dynamic_slice_in_dim(field, core * columns, columns, 1)

    start = all_rows(mine(inputs))
    upstream = all_rows(mine(cotangent))
    first_out, first_stored = forward_section(start, extend_local(start), first_params)
    second_out, second_stored = forward_section(first_out, extend_local(first_out), second_params)
    second_grad, second_pairs, second_small = backward_section(
        second_stored, upstream, second_params, extend_local
    )
    second_sums = section_sums(second_pairs, second_small, 1)
    first_grad, first_pairs, first_small = backward_section(
        first_stored, second_grad, first_params, extend_local
    )
    first_sums = section_sums(first_pairs, first_small, 0)

    def whole_tile(earlier, latter):
        band = lax.axis_index("lat") * rows
        earlier = lax.dynamic_slice_in_dim(earlier, band, rows, 0)
        latter = lax.dynamic_slice_in_dim(latter, band, rows, 0)
        kept = jnp.where(leading, earlier, latter)
        came = other_core(jnp.where(leading, latter, earlier))
        west = jnp.where(leading, kept, came)
        east = jnp.where(leading, came, kept)
        return jnp.concatenate([west, east], axis=1)[None]

    section_out = whole_tile(first_out, second_out)
    boundary_grad = whole_tile(first_grad, second_grad)
    chosen = jax.tree.map(
        lambda earlier, latter: jnp.where(leading, earlier, latter)[None], first_sums, second_sums
    )
    return (section_out, boundary_grad) + chosen


def solution(mesh):
    placed = (
        P(("groups", "lat"), "lon", None),
        P(("groups", "lat"), "lon", None),
        P("segment", None, None),
        P("segment", None),
        P("segment", None),
        P("segment", None),
        P("segment", None, None),
        P("segment", None),
        P("segment", None, None),
        P("segment", None),
        P("segment", None),
    )
    return jax.shard_map(
        local,
        mesh=mesh,
        in_specs=placed,
        out_specs=(
            P("segment", ("groups", "lat"), "lon", None),
            P("segment", ("groups", "lat"), "lon", None),
            P(("groups", "segment"), None, ("lon", "lat")),
            P(("groups", "segment"), ("lon", "lat"), None),
            P(("groups", "segment"), ("lon", "lat")),
            P(("groups", "segment"), None, ("lon", "lat")),
            P(("groups", "segment"), None, ("lon", "lat")),
        ),
        check_vma=False,
    )
```

```python
import functools

import jax
import jax.numpy as jnp
from jax import lax
from jax.experimental import pallas as pl
from jax.experimental.pallas import tpu as pltpu
from jax.sharding import PartitionSpec as P

KERNEL = 7
MARGIN = KERNEL // 2
LANES = 128
SUBLANES = 8
EPSILON = 1e-06
ROOT_HALF = 0.7071067811865476
DENSITY_SCALE = 0.3989422804014327
RING = ("lon", "segment")
VMEM_BYTES = 48 * 1024 * 1024

TAPS = KERNEL * KERNEL
CONV_BIAS, GAIN, SHIFT, OUT_BIAS, SCALING, HIDDEN_BIAS = range(TAPS, TAPS + 6)


def gelu_parts(before):
    cumulative = 0.5 * (1.0 + lax.erf(before * ROOT_HALF))
    density = jnp.exp(-0.5 * before * before) * DENSITY_SCALE
    return (before * cumulative, cumulative + before * density)


def fill_padded(padded, field, west, east, beyond, beyond_west, beyond_east):
    rows, columns = field.shape[:2]
    inner = slice(MARGIN, MARGIN + columns)
    outer = slice(MARGIN + columns, 2 * MARGIN + columns)
    here = slice(MARGIN, MARGIN + rows)
    padded[here, inner] = field[...].astype(jnp.float32)
    padded[here, :MARGIN] = west[...].astype(jnp.float32)
    padded[here, outer] = east[...].astype(jnp.float32)
    for depth in range(MARGIN):
        for target, source in (
            (MARGIN - 1 - depth, depth),
            (MARGIN + rows + depth, 2 * MARGIN - 1 - depth),
        ):
            padded[target, inner] = beyond[source].astype(jnp.float32)
            padded[target, :MARGIN] = beyond_west[source].astype(jnp.float32)
            padded[target, outer] = beyond_east[source].astype(jnp.float32)


def row_blocks(rows):
    size = 16 if rows % 16 == 0 else 8
    return [(start, size) for start in range(0, rows, size)]


def tap_window(padded, start, size, col_tap, col_tile, lanes):
    first = col_tile * SUBLANES + col_tap
    return padded[start : start + size + 2 * MARGIN, first : first + SUBLANES, lanes]


def correlate(result, padded, small, folded):
    rows, columns, channels = result.shape

    def channel_group(group, carry):
        lanes = pl.ds(pl.multiple_of(group * LANES, LANES), LANES)
        for start, size in row_blocks(rows):
            for col_tile in range(columns // SUBLANES):
                total = jnp.zeros((size, SUBLANES, LANES), jnp.float32)
                for col_tap in range(KERNEL):
                    window = tap_window(padded, start, size, col_tap, col_tile, lanes)
                    col = KERNEL - 1 - col_tap if folded else col_tap
                    taps = [
                        small[pl.ds(row * KERNEL + col, 1), lanes][None] for row in range(KERNEL)
                    ]
                    for row_tap in range(KERNEL):
                        seen = window[row_tap : row_tap + size]
                        if not folded:
                            total = total + seen * taps[row_tap]
                            continue
                        north = max(0, MARGIN - row_tap) if start == 0 else 0
                        south = max(0, row_tap - MARGIN) if start + size == rows else 0
                        pieces = []
                        if north:
                            pieces.append(seen[:north] * taps[row_tap])
                        pieces.append(seen[north : size - south] * taps[KERNEL - 1 - row_tap])
                        if south:
                            pieces.append(seen[size - south :] * taps[row_tap])
                        total = total + jnp.concatenate(pieces, axis=0)
                tile = slice(col_tile * SUBLANES, (col_tile + 1) * SUBLANES)
                result[start : start + size, tile, lanes] = total
        return carry

    lax.fori_loop(0, channels // LANES, channel_group, 0)


def tap_sums(result, padded, grad):
    rows, columns, channels = grad.shape

    def channel_group(group, carry):
        lanes = pl.ds(pl.multiple_of(group * LANES, LANES), LANES)
        for col_tap in range(KERNEL):
            totals = [jnp.zeros((SUBLANES, LANES), jnp.float32)] * KERNEL
            for start, size in row_blocks(rows):
                for col_tile in range(columns // SUBLANES):
                    window = tap_window(padded, start, size, col_tap, col_tile, lanes)
                    tile = slice(col_tile * SUBLANES, (col_tile + 1) * SUBLANES)
                    here = grad[start : start + size, tile, lanes]
                    for row_tap in range(KERNEL):
                        totals[row_tap] = totals[row_tap] + jnp.sum(
                            here * window[row_tap : row_tap + size], axis=0
                        )
            for row_tap in range(KERNEL):
                result[pl.ds(row_tap * KERNEL + col_tap, 1), lanes] = jnp.sum(
                    totals[row_tap], axis=0, keepdims=True
                )
        return carry

    lax.fori_loop(0, channels // LANES, channel_group, 0)


def over_cells(cells, step, body, init):
    def one(index, carry):
        return body(pl.ds(pl.multiple_of(index * step, step), step), carry)

    return lax.fori_loop(0, cells // step, one, init)


def normalise(activity, small, unit_norm, inverse, normed):
    def body(cells, carry):
        value = activity[cells] + small[CONV_BIAS : CONV_BIAS + 1]
        centred = value - jnp.mean(value, axis=-1, keepdims=True)
        variance = jnp.mean(centred * centred, axis=-1, keepdims=True)
        scale = lax.rsqrt(variance + EPSILON)
        unit = centred * scale
        unit_norm[cells] = unit
        inverse[cells] = scale
        normed[cells] = (unit * small[GAIN : GAIN + 1] + small[SHIFT : SHIFT + 1]).astype(
            jnp.bfloat16
        )
        return carry

    over_cells(activity.shape[0], 32, body, 0)


def hidden_chunks(small, units):
    channels = small.shape[1]
    return [
        (slice(part * channels, (part + 1) * channels), small[HIDDEN_BIAS + part : HIDDEN_BIAS + part + 1])
        for part in range(units // channels)
    ]


def mlp_forward(field, normed, up, down, small, before, hidden, slope, branch, result):
    cells, units = hidden.shape
    for part, bias in hidden_chunks(small, units):
        before[...] = jnp.dot(normed[...], up[:, part], preferred_element_type=jnp.float32) + bias

        def body(rows, carry):
            activated, slope_value = gelu_parts(before[rows])
            hidden[rows, part] = activated.astype(jnp.bfloat16)
            slope[rows, part] = slope_value.astype(jnp.bfloat16)
            return carry

        over_cells(cells, 32, body, 0)
    branch[...] = (
        jnp.dot(hidden[...], down[...], preferred_element_type=jnp.float32)
        + small[OUT_BIAS : OUT_BIAS + 1]
    )
    flat = field[...].astype(jnp.float32).reshape(cells, -1)
    summed = flat + small[SCALING : SCALING + 1] * branch[...]
    result[...] = summed.astype(jnp.bfloat16).reshape(result.shape)


def mlp_backward(upstream, up, down, small, saved, before_grad, scaled, act_grad, sums, bias_sum):
    unit_norm, inverse, slope, branch, wide = saved
    cells, units = before_grad.shape
    contract_last = (((1,), (1,)), ((), ()))
    incoming = upstream[...].astype(jnp.float32).reshape(cells, -1)
    low = (incoming * small[SCALING : SCALING + 1]).astype(jnp.bfloat16)
    scaled[...] = low
    sums[3:4] = jnp.sum(low.astype(jnp.float32), axis=0, keepdims=True)
    sums[4:5] = jnp.sum(incoming * branch[...], axis=0, keepdims=True)
    for part, _ in hidden_chunks(small, units):
        hidden_grad = lax.dot_general(
            scaled[...], down[part], contract_last, preferred_element_type=jnp.float32
        )
        low = (hidden_grad * slope[:, part].astype(jnp.float32)).astype(jnp.bfloat16)
        before_grad[:, part] = low
        bias_sum[:, part] = jnp.sum(low.astype(jnp.float32), axis=0, keepdims=True)
    wide[...] = lax.dot_general(
        before_grad[...], up[...], contract_last, preferred_element_type=jnp.float32
    )
    step = 32
    columns = act_grad.shape[1]
    zeros = jnp.zeros((SUBLANES, wide.shape[1]), jnp.float32)

    def fold(value):
        return jnp.sum(value.reshape(-1, SUBLANES, value.shape[1]), axis=0)

    def body(rows, carry):
        shift_sum, gain_sum, bias = carry
        normed_grad = wide[rows]
        unit = unit_norm[rows]
        gained = normed_grad * small[GAIN : GAIN + 1]
        weighted = gained * unit
        grad = inverse[rows] * (
            gained
            - jnp.mean(gained, axis=-1, keepdims=True)
            - unit * jnp.mean(weighted, axis=-1, keepdims=True)
        )
        rounded = grad.astype(jnp.bfloat16).astype(jnp.float32)
        wide[rows] = rounded
        return (shift_sum + fold(normed_grad), gain_sum + fold(normed_grad * unit), bias + fold(rounded))

    shift_sum, gain_sum, bias = over_cells(cells, step, body, (zeros, zeros, zeros))
    sums[0:1] = jnp.sum(bias, axis=0, keepdims=True)
    sums[1:2] = jnp.sum(gain_sum, axis=0, keepdims=True)
    sums[2:3] = jnp.sum(shift_sum, axis=0, keepdims=True)
    act_grad[...] = wide[...].astype(jnp.bfloat16).reshape(act_grad.shape)


def fetch(own, flag, mine, theirs, buffers, sems):
    for index, buffer in enumerate(buffers):

        @pl.when(flag[0] == own)
        def _():
            pltpu.make_async_copy(mine[index], buffer, sems.at[index]).start()

        @pl.when(flag[0] != own)
        def _():
            pltpu.make_async_copy(theirs[index], buffer, sems.at[index]).start()


def arrived(mine, buffers, sems, index):
    pltpu.make_async_copy(mine[index], buffers[index], sems.at[index]).wait()


def first_forward_kernel(
    flag, small, field, west, east, beyond, beyond_west, beyond_east,
    up_mine, down_mine, up_theirs, down_theirs,
    result, unit_norm, inverse, normed, hidden, slope, branch,
    padded, activity, before, up, down, sems,
):
    mine, theirs, buffers = (up_mine, down_mine), (up_theirs, down_theirs), (up, down)
    fetch(0, flag, mine, theirs, buffers, sems)
    fill_padded(padded, field, west, east, beyond, beyond_west, beyond_east)
    correlate(activity, padded, small, False)
    flat = activity.reshape(normed.shape)
    normalise(flat, small, unit_norm, inverse, normed)
    arrived(mine, buffers, sems, 0)
    arrived(mine, buffers, sems, 1)
    mlp_forward(field, normed, up, down, small, before, hidden, slope, branch, result)


def second_section_kernel(
    flag, small, field, west, east, beyond, beyond_west, beyond_east, upstream,
    up_mine, down_mine, up_theirs, down_theirs,
    result, normed, hidden, before_grad, scaled, act_grad, sums, bias_sum,
    padded, activity, before, up, down, unit_norm, inverse, slope, branch, sems,
):
    mine, theirs, buffers = (up_mine, down_mine), (up_theirs, down_theirs), (up, down)
    fetch(1, flag, mine, theirs, buffers, sems)
    fill_padded(padded, field, west, east, beyond, beyond_west, beyond_east)
    correlate(activity, padded, small, False)
    flat = activity.reshape(normed.shape)
    normalise(flat, small, unit_norm, inverse, normed)
    arrived(mine, buffers, sems, 0)
    arrived(mine, buffers, sems, 1)
    mlp_forward(field, normed, up, down, small, before, hidden, slope, branch, result)
    saved = (unit_norm, inverse, slope, branch, flat)
    mlp_backward(upstream, up, down, small, saved, before_grad, scaled, act_grad, sums, bias_sum)


def tap_sums_kernel(
    grad, field, west, east, beyond, beyond_west, beyond_east, result, padded, wide
):
    fill_padded(padded, field, west, east, beyond, beyond_west, beyond_east)
    wide[...] = grad[...].astype(jnp.float32)
    tap_sums(result, padded, wide)


def pass_back(small, upstream, act_grad, halos, padded, through, result):
    fill_padded(padded, act_grad, *halos)
    correlate(through, padded, small, True)
    result[...] = (upstream[...].astype(jnp.float32) + through[...]).astype(jnp.bfloat16)


def first_backward_kernel(
    flag, small_second, small, upstream, act_grad, west, east, beyond, beyond_west, beyond_east,
    unit_norm, inverse, slope, branch, up_mine, down_mine, up_theirs, down_theirs,
    passed, before_grad, scaled, first_grad, sums, bias_sum,
    padded, through, up, down, sems,
):
    mine, theirs, buffers = (up_mine, down_mine), (up_theirs, down_theirs), (up, down)
    fetch(0, flag, mine, theirs, buffers, sems)
    halos = (west, east, beyond, beyond_west, beyond_east)
    pass_back(small_second, upstream, act_grad, halos, padded, through, passed)
    arrived(mine, buffers, sems, 0)
    arrived(mine, buffers, sems, 1)
    saved = (unit_norm, inverse, slope, branch, through.reshape(scaled.shape))
    mlp_backward(passed, up, down, small, saved, before_grad, scaled, first_grad, sums, bias_sum)


def last_pass_kernel(
    small, upstream, act_grad, west, east, beyond, beyond_west, beyond_east, result, padded, through
):
    halos = (west, east, beyond, beyond_west, beyond_east)
    pass_back(small, upstream, act_grad, halos, padded, through, result)


def on_core(kernel, operands, outs, scratch, flops):
    return pl.pallas_call(
        kernel,
        out_shape=[jax.ShapeDtypeStruct(shape, kind) for shape, kind in outs],
        in_specs=[pl.BlockSpec(memory_space=space) for _, space in operands],
        out_specs=[pl.BlockSpec(memory_space=pltpu.VMEM) for _ in outs],
        scratch_shapes=scratch,
        compiler_params=pltpu.CompilerParams(vmem_limit_bytes=VMEM_BYTES),
        cost_estimate=pl.CostEstimate(flops=flops, bytes_accessed=1 << 20, transcendentals=0),
    )(*[array for array, _ in operands])


def in_vmem(*arrays):
    return [(array, pltpu.VMEM) for array in arrays]


def in_hbm(*arrays):
    return [(array, pl.ANY) for array in arrays]


def padded_scratch(field):
    rows, columns, channels = field.shape
    wide = -(-(columns + 2 * MARGIN) // SUBLANES) * SUBLANES
    return pltpu.VMEM((rows + 2 * MARGIN, wide, channels), jnp.float32)


def weight_scratch(weights):
    up, down = weights
    return [pltpu.VMEM(up.shape, up.dtype), pltpu.VMEM(down.shape, down.dtype)]


def sizes(field, weights):
    rows, columns, channels = field.shape
    return rows * columns, channels, weights[0].shape[1]


def first_forward(flag, small, field, halos, mine, theirs):
    cells, channels, units = sizes(field, mine)
    low, full = jnp.bfloat16, jnp.float32
    return on_core(
        first_forward_kernel,
        [(flag, pltpu.SMEM)] + in_vmem(small, field, *halos) + in_hbm(*mine, *theirs),
        [
            (field.shape, low),
            ((cells, channels), full),
            ((cells, 1), full),
            ((cells, channels), low),
            ((cells, units), low),
            ((cells, units), low),
            ((cells, channels), full),
        ],
        [
            padded_scratch(field),
            pltpu.VMEM(field.shape, full),
            pltpu.VMEM((cells, channels), full),
            *weight_scratch(mine),
            pltpu.SemaphoreType.DMA((2,)),
        ],
        4 * cells * channels * units,
    )


def second_section(flag, small, field, halos, upstream, mine, theirs):
    cells, channels, units = sizes(field, mine)
    low, full = jnp.bfloat16, jnp.float32
    return on_core(
        second_section_kernel,
        [(flag, pltpu.SMEM)] + in_vmem(small, field, *halos, upstream) + in_hbm(*mine, *theirs),
        [
            (field.shape, low),
            ((cells, channels), low),
            ((cells, units), low),
            ((cells, units), low),
            ((cells, channels), low),
            (field.shape, low),
            ((5, channels), full),
            ((1, units), full),
        ],
        [
            padded_scratch(field),
            pltpu.VMEM(field.shape, full),
            pltpu.VMEM((cells, channels), full),
            *weight_scratch(mine),
            pltpu.VMEM((cells, channels), full),
            pltpu.VMEM((cells, 1), full),
            pltpu.VMEM((cells, units), low),
            pltpu.VMEM((cells, channels), full),
            pltpu.SemaphoreType.DMA((2,)),
        ],
        12 * cells * channels * units,
    )


def tap_gradient(grad, field, halos):
    channels = field.shape[2]
    return on_core(
        tap_sums_kernel,
        in_vmem(grad, field, *halos),
        [((TAPS, channels), jnp.float32)],
        [padded_scratch(field), pltpu.VMEM(field.shape, jnp.float32)],
        2 * TAPS * field.size,
    )[0]


def first_backward(flag, small_second, small, upstream, act_grad, halos, saved, mine, theirs):
    cells, channels, units = sizes(act_grad, mine)
    low, full = jnp.bfloat16, jnp.float32
    return on_core(
        first_backward_kernel,
        [(flag, pltpu.SMEM)]
        + in_vmem(small_second, small, upstream, act_grad, *halos, *saved)
        + in_hbm(*mine, *theirs),
        [
            (act_grad.shape, low),
            ((cells, units), low),
            ((cells, channels), low),
            (act_grad.shape, low),
            ((5, channels), full),
            ((1, units), full),
        ],
        [
            padded_scratch(act_grad),
            pltpu.VMEM(act_grad.shape, full),
            *weight_scratch(mine),
            pltpu.SemaphoreType.DMA((2,)),
        ],
        8 * cells * channels * units,
    )


def last_pass(small, upstream, act_grad, halos):
    return on_core(
        last_pass_kernel,
        in_vmem(small, upstream, act_grad, *halos),
        [(act_grad.shape, jnp.bfloat16)],
        [padded_scratch(act_grad), pltpu.VMEM(act_grad.shape, jnp.float32)],
        2 * TAPS * act_grad.size,
    )[0]


def from_ahead(value, axis, steps):
    count = lax.axis_size(axis)
    return lax.ppermute(value, axis, [((i + steps) % count, i) for i in range(count)])


def all_rows(band):
    count = lax.axis_size("lat")
    here = lax.axis_index("lat")
    rows = band.shape[0]
    whole = jnp.zeros((count * rows,) + band.shape[1:], band.dtype)
    for steps in range(count):
        piece = band if steps == 0 else from_ahead(band, "lat", steps)
        whole = lax.dynamic_update_slice_in_dim(whole, piece, (here + steps) % count * rows, 0)
    return whole


def halo(values):
    half = lax.axis_size(RING) // 2
    polar = jnp.concatenate([values[:MARGIN], values[-MARGIN:]], axis=0)
    return (
        from_ahead(values[:, -MARGIN:], RING, -1),
        from_ahead(values[:, :MARGIN], RING, 1),
        from_ahead(polar, RING, half),
        from_ahead(polar[:, -MARGIN:], RING, half - 1),
        from_ahead(polar[:, :MARGIN], RING, half + 1),
    )


def other_core(value):
    return lax.ppermute(value, "segment", [(0, 1), (1, 0)])


def own_blocks(sums, blocks):
    lons, lats = lax.axis_size("lon"), lax.axis_size("lat")
    cut = sums.reshape(sums.shape[:-1] + (lons, lats, blocks))
    return lax.dynamic_index_in_dim(cut, lax.axis_index("lat"), cut.ndim - 2, keepdims=False)


def sum_to_owner(partial, section):
    lons = lax.axis_size("lon")
    here = lax.axis_index("lon")
    kind = partial.dtype
    other = lax.ppermute(partial, "segment", [(1 - section, section)])
    chip = partial.astype(jnp.float32) + other.astype(jnp.float32)
    low = chip.astype(kind)
    total = lax.dynamic_index_in_dim(chip, here, 1, keepdims=False)
    for steps in range(1, lons):
        block = lax.dynamic_index_in_dim(low, (here + steps) % lons, 1, keepdims=False)
        pairs = [
            (i * 2 + section, (i + steps) % lons * 2 + section) for i in range(lons)
        ]
        total = total + lax.ppermute(block, RING, pairs).astype(jnp.float32)
    return total


def cell_products(left, right):
    cells, lons, wide = right.shape
    sums = jnp.dot(left.T, right.reshape(cells, -1), preferred_element_type=jnp.float32)
    return sums.astype(jnp.bfloat16).reshape(-1, lons, wide)


def section_sums(matrices, smalls, section):
    normed, hidden, before_grad, scaled = matrices
    stencil_sum, vectors, bias_sum = smalls
    devices = lax.axis_size("lon") * lax.axis_size("lat")
    channels, units = normed.shape[1], hidden.shape[1]
    wide, narrow = units // devices, channels // devices
    down = sum_to_owner(
        cell_products(scaled, own_blocks(hidden, wide)),
        section,
    )
    up = sum_to_owner(
        cell_products(normed, own_blocks(before_grad, wide)),
        section,
    )
    thin = own_blocks(jnp.concatenate([stencil_sum, vectors], axis=0), narrow)
    bias = own_blocks(bias_sum, wide).reshape(thin.shape[1], -1, narrow).transpose(1, 0, 2)
    small = sum_to_owner(jnp.concatenate([thin, bias], axis=0), section)
    taps = stencil_sum.shape[0]
    rows = taps + vectors.shape[0]
    return (up, down.T, small[rows:].reshape(-1), small[:taps], small[taps:rows])


def local(
    inputs,
    cotangent,
    kernel,
    conv_bias,
    norm_gain,
    norm_shift,
    up_weight,
    hidden_bias,
    down_weight,
    out_bias,
    layer_scale,
):
    core = lax.axis_index("segment")
    leading = core == 0
    columns = inputs.shape[1] // 2
    rows = inputs.shape[0]
    flag = core.astype(jnp.int32).reshape(1)
    small_mine = jnp.concatenate(
        [
            kernel[0].astype(jnp.float32),
            conv_bias,
            norm_gain,
            norm_shift,
            out_bias,
            layer_scale,
            hidden_bias.reshape(-1, kernel.shape[2]),
        ],
        axis=0,
    )
    small_theirs = other_core(small_mine)
    small_first = jnp.where(leading, small_mine, small_theirs)
    small_second = jnp.where(leading, small_theirs, small_mine)
    weights = (up_weight[0], down_weight[0])
    others = (other_core(up_weight[0]), other_core(down_weight[0]))

    def mine(field):
        return lax.dynamic_slice_in_dim(field, core * columns, columns, 1)

    start = all_rows(mine(inputs))
    upstream = all_rows(mine(cotangent))
    start_halo = halo(start)
    first_out, unit_norm, inverse, normed, hidden, slope, branch = first_forward(
        flag, small_first, start, start_halo, weights, others
    )
    middle_halo = halo(first_out)
    second_out, *second_pairs, second_act, second_vectors, second_bias = second_section(
        flag, small_second, first_out, middle_halo, upstream, weights, others
    )
    second_halo = halo(second_act)
    second_taps = tap_gradient(second_act, first_out, middle_halo)
    second_sums = section_sums(second_pairs, (second_taps, second_vectors, second_bias[0]), 1)
    second_grad, before_grad, scaled, first_act, first_vectors, first_bias = first_backward(
        flag,
        small_second,
        small_first,
        upstream,
        second_act,
        second_halo,
        (unit_norm, inverse, slope, branch),
        weights,
        others,
    )
    first_halo = halo(first_act)
    first_taps = tap_gradient(first_act, start, start_halo)
    first_sums = section_sums(
        (normed, hidden, before_grad, scaled), (first_taps, first_vectors, first_bias[0]), 0
    )
    first_grad = last_pass(small_first, second_grad, first_act, first_halo)

    def whole_tile(earlier, latter):
        band = lax.axis_index("lat") * rows
        earlier = lax.dynamic_slice_in_dim(earlier, band, rows, 0)
        latter = lax.dynamic_slice_in_dim(latter, band, rows, 0)
        kept = jnp.where(leading, earlier, latter)
        came = other_core(jnp.where(leading, latter, earlier))
        west = jnp.where(leading, kept, came)
        east = jnp.where(leading, came, kept)
        return jnp.concatenate([west, east], axis=1)[None]

    section_out = whole_tile(first_out, second_out)
    boundary_grad = whole_tile(first_grad, second_grad)
    chosen = jax.tree.map(
        lambda earlier, latter: jnp.where(leading, earlier, latter)[None], first_sums, second_sums
    )
    return (section_out, boundary_grad) + chosen


def solution(mesh):
    placed = (
        P(("groups", "lat"), "lon", None),
        P(("groups", "lat"), "lon", None),
        P("segment", None, None),
        P("segment", None),
        P("segment", None),
        P("segment", None),
        P("segment", None, None),
        P("segment", None),
        P("segment", None, None),
        P("segment", None),
        P("segment", None),
    )
    return jax.shard_map(
        local,
        mesh=mesh,
        in_specs=placed,
        out_specs=(
            P("segment", ("groups", "lat"), "lon", None),
            P("segment", ("groups", "lat"), "lon", None),
            P(("groups", "segment"), None, ("lon", "lat")),
            P(("groups", "segment"), ("lon", "lat"), None),
            P(("groups", "segment"), ("lon", "lat")),
            P(("groups", "segment"), None, ("lon", "lat")),
            P(("groups", "segment"), None, ("lon", "lat")),
        ),
        check_vma=False,
    )
```
